256 devices in a mesh: wide: 16 (over y, z_lo, core), narrow: 16 (over z_hi, x).
Axes of the slice: x: 4, y: 4, z: 8 (z_hi: 4, z_lo: 2; z = z_hi * 2 + z_lo), core: 2. Of those that a mesh axis runs over, the one named last changes fastest.
Arguments:
- snapshots: bfloat16 [786432, 512], P(('wide', 'narrow')), as said below
- range_test: bfloat16 [512, 384], replicated, may hold values from -0.25 to 0.25
- corange_test: bfloat16 [786432, 768], P(('wide', 'narrow')), may hold values from -0.02734375 to 0.02734375
Outputs:
- basis: float32 [786432, 384], P(('wide', 'narrow'))
- cosketch: float32 [768, 512], P('wide', 'narrow')
The draws below stay inside these ranges and needn't reach their ends.
Inputs may be any that keep to these rules, and one draw needn't show every extreme that they name: `snapshots`: snapshot values are finite and of order one to some tens.
All inputs are finite; a program needn't handle non-finite values.
Results may differ from the reference program's by a relative error of at most 0.0003.
Values sent between devices are 32-bit elements; how exact they have to be, the bound alone decides.
No kernel may reach another device: no remote copies, remote signals or barrier semaphores. Data moves between devices by JAX's collectives and lax.ppermute only.
A program may use at most 128 MiB of HBM per device.

```python
import math
import jax
import jax.numpy as jnp
from jax import lax

SNAPS = 512
RANK = 384
CORANGE = 768
TOTAL_ROWS = 786432


def draw_snapshots(key, part):
    key = jax.random.fold_in(key, 7)
    keys = jax.random.split(key, 3)
    row_scale = jnp.exp(jax.random.uniform(keys[0], (TOTAL_ROWS, 1), jnp.float32) * math.log(10.0)) / 4.0
    col_scale = jnp.exp(jax.random.uniform(keys[1], (1, SNAPS), jnp.float32) * math.log(10.0)) / 4.0
    base = jax.random.normal(keys[2], (TOTAL_ROWS, SNAPS), jnp.float32)
    return (base * row_scale * col_scale).astype(jnp.bfloat16)


def spiked(result, own_key, source, target, parts, factor):
    owner, partner = [(jnp.arange(result.shape[axis_at]) // (result.shape[axis_at] // parts)).reshape([-1 if axis == axis_at else 1 for axis in range(result.ndim)]) for axis_at in (source, target)]
    chosen = jax.random.permutation(own_key, parts)[partner]
    strong = (owner == chosen) | (owner == (partner + parts // 2) % parts)
    return jnp.where(strong, factor * result, result)


def steps_of(key, shape, cuts, low, largest):
    gain, own = 1.0, jax.random.fold_in(key, 6)
    for dim, blocks in cuts:
        heights = jnp.exp(jax.random.uniform(jax.random.fold_in(own, dim), (blocks,), jnp.float32, low / len(cuts), largest / len(cuts)))
        gain = gain * jnp.repeat(heights, shape[dim] // blocks).reshape([-1 if axis == dim else 1 for axis in range(len(shape))])
    return gain


def bell_draw(key, shape, spread, bound, cuts=(), held_as=jnp.bfloat16):
    values = spread * jax.random.normal(key, shape, jnp.float32)
    if cuts:
        values = values * steps_of(key, shape, cuts, -0.22, 0.18)
    return jnp.clip(values, -bound, bound).astype(held_as)


def gaussian_with(rng, dims, spread, most, cuts, heavy, kind=jnp.bfloat16):
    drawn = spread * jax.random.normal(rng, dims, jnp.float32)
    if cuts:
        drawn = drawn * steps_of(rng, dims, cuts, -0.22, 0.18)
    return jnp.clip(spiked(drawn, jax.random.fold_in(rng, 3), *heavy), -most, most).astype(kind)


def setup_inputs(seed: int = 0) -> dict:
    arg_keys = jax.random.split(jax.random.key(seed), 4)
    snapshots = draw_snapshots(jax.random.fold_in(arg_keys[3], 71), 0)
    range_test = bell_draw(arg_keys[1], (SNAPS, RANK), SNAPS ** -0.5, 0.25)
    corange_test = gaussian_with(arg_keys[2], (TOTAL_ROWS, CORANGE), TOTAL_ROWS ** -0.5, 0.02734375, ((0, 256),), (0, 1, 256, 6.0))
    return dict(snapshots=snapshots, range_test=range_test, corange_test=corange_test)


def reference(snapshots, range_test, corange_test):
    sketch = jnp.dot(snapshots.astype(jnp.float32), range_test.astype(jnp.float32), preferred_element_type=jnp.float32)
    gram = jnp.dot(sketch.T, sketch, precision=lax.Precision.HIGHEST)
    lower = jnp.linalg.cholesky(gram)
    solved = lax.linalg.triangular_solve(lower, sketch, left_side=False, lower=True, transpose_a=True)
    basis = solved * jnp.sqrt(jnp.float32(TOTAL_ROWS))
    cosketch = jnp.dot(corange_test.T.astype(jnp.float32), snapshots.astype(jnp.float32), preferred_element_type=jnp.float32)
    return (basis, cosketch)
```

```python
import jax
import jax.numpy as jnp
from jax import lax
from jax.experimental import pallas as pl
from jax.experimental.pallas import tpu as pltpu
from jax.sharding import Mesh, PartitionSpec as P

F32 = jnp.float32
BF16 = jnp.bfloat16
ROWS = ("y", "zl", "core", "zh", "x")
PLANE = ("y", "x")
COLUMN = ("zl", "zh")
VMEM = pl.BlockSpec(memory_space=pltpu.VMEM)
ANY = pl.BlockSpec(memory_space=pl.ANY)
CONTRACT0 = (((0,), (0,)), ((), ()))
BLOCKS = ((0, 0), (0, 1), (0, 2), (1, 1), (1, 2), (2, 2))


def split(value, parts):
    pieces = []
    for _ in range(parts):
        piece = value.astype(BF16)
        pieces.append(piece)
        value = value - piece.astype(F32)
    return pieces


def lanes(shape):
    return lax.broadcasted_iota(jnp.int32, shape, len(shape) - 1)


def products_kernel(x_ref, c_ref, r_ref, mine_ref, other_ref, s_acc, k_acc, g_acc, p_acc):
    step = pl.program_id(0)
    x = x_ref[...]
    s = lax.dot_general(x, x, CONTRACT0, preferred_element_type=F32)
    k = lax.dot_general(c_ref[...], x, CONTRACT0, preferred_element_type=F32)

    @pl.when(step == 0)
    def _():
        s_acc[...] = s
        k_acc[...] = k

    @pl.when(step > 0)
    def _():
        s_acc[...] += s
        k_acc[...] += k

    @pl.when(step == pl.num_programs(0) - 1)
    def _():
        r = r_ref[...]
        t = sum(jnp.dot(p, r, preferred_element_type=F32) for p in split(s_acc[...], 3))
        pieces = split(t, 3)
        at = 0
        for i in range(3):
            left = r[:, i * 128 : (i + 1) * 128]
            row = sum(
                lax.dot_general(left, p[:, i * 128 :], CONTRACT0, preferred_element_type=F32)
                for p in pieces
            )
            for j in range(3 - i):
                g_acc[at * 128 : (at + 1) * 128, :] = row[:, j * 128 : (j + 1) * 128]
                at += 1
        quarter = lanes((768, 128)) // 32
        for n in range(4):
            out = jnp.zeros((768, 128), F32)
            for zh in range(4):
                piece = k_acc[:, zh * 128 : (zh + 1) * 128]
                shift = ((zh - n) * 32) % 128
                if shift:
                    piece = pltpu.roll(piece, shift, 1)
                out = jnp.where(quarter == zh, piece, out)
            p_acc[n] = out
        core = lax.axis_index("core")
        for side, ref in ((core, mine_ref), (1 - core, other_ref)):
            for y in range(4):
                for n in range(4):
                    peer = y * 4 + n
                    ref[peer, 0:24, :] = g_acc[pl.ds(pl.multiple_of(side * 384 + peer * 24, 8), 24), :]
                    for zl in range(2):
                        start = pl.multiple_of((y * 4 + zl * 2 + side) * 48, 8)
                        ref[peer, 24 + zl * 48 : 72 + zl * 48, :] = p_acc[n, pl.ds(start, 48), :]


def products(x, c, r):
    tile = 1024
    half = jax.ShapeDtypeStruct((16, 120, 128), F32)
    whole = pl.BlockSpec((16, 120, 128), lambda i: (0, 0, 0))
    return pl.pallas_call(
        products_kernel,
        grid=(x.shape[0] // tile,),
        in_specs=[
            pl.BlockSpec((tile, 512), lambda i: (i, 0)),
            pl.BlockSpec((tile, 768), lambda i: (i, 0)),
            pl.BlockSpec((512, 384), lambda i: (0, 0)),
        ],
        out_specs=(whole, whole),
        out_shape=(half, half),
        scratch_shapes=[
            pltpu.VMEM((512, 512), F32),
            pltpu.VMEM((768, 512), F32),
            pltpu.VMEM((768, 128), F32),
            pltpu.VMEM((4, 768, 128), F32),
        ],
        compiler_params=pltpu.CompilerParams(vmem_limit_bytes=48 << 20),
    )(x, c, r)


def column_kernel(got_ref, out_ref):
    total = got_ref[0]
    for i in range(1, 16):
        total = total + got_ref[i]
    gram = total[0:24]
    lane = lanes((16, 128)) // 32
    for zl in range(2):
        for zh in range(4):
            peer = zl * 4 + zh
            out_ref[peer, 0:24, :] = gram
            out = jnp.zeros((16, 128), F32)
            for q in range(3):
                start = 24 + zl * 48 + q * 16
                piece = total[start : start + 16]
                shift = ((q - zh) * 32) % 128
                if shift:
                    piece = pltpu.roll(piece, shift, 1)
                out = jnp.where(lane == q, piece, out)
            out_ref[peer, 24:40, :] = out


def column_blocks(got):
    return pl.pallas_call(
        column_kernel,
        in_specs=[VMEM],
        out_specs=VMEM,
        out_shape=jax.ShapeDtypeStruct((8, 40, 128), F32),
    )(got)


def plane_kernel(got_ref, gram_ref, cosketch_ref):
    total = got_ref[0]
    for i in range(1, 8):
        total = total + got_ref[i]
    for i in range(16):
        gram_ref[i] = total[0:24]
    for q in range(3):
        piece = total[24:40]
        if q:
            piece = pltpu.roll(piece, 128 - q * 32, 1)
        cosketch_ref[q * 16 : (q + 1) * 16, :] = piece[:, 0:32]


def plane_blocks(got):
    return pl.pallas_call(
        plane_kernel,
        in_specs=[VMEM],
        out_specs=(VMEM, VMEM),
        out_shape=(
            jax.ShapeDtypeStruct((16, 24, 128), F32),
            jax.ShapeDtypeStruct((48, 32), F32),
        ),
    )(got)


def spread(value):
    return jnp.broadcast_to(value, (8, 128))


def inverse_factor(block):
    n = 16
    d = [block[8 * i : 8 * i + 8, :] for i in range(n)]
    row = lax.broadcasted_iota(jnp.int32, (8, 128), 0)
    lane = lanes((8, 128))
    v = [jnp.where(lane == row + 8 * i, 1.0, 0.0).astype(F32) for i in range(n)]
    for p in range(n):
        columns = [spread(d[p][:, 8 * p + j : 8 * p + j + 1]) for j in range(8)]
        s = [[spread(columns[j][k : k + 1, :]) if k >= j else None for j in range(8)] for k in range(8)]
        r = []
        for j in range(8):
            r.append(lax.rsqrt(s[j][j]))
            for k in range(j + 1, 8):
                s[k][j] = s[k][j] * r[j]
            for m in range(j + 1, 8):
                for k in range(m, 8):
                    s[k][m] = s[k][m] - s[k][j] * s[m][j]

        def forward(rows):
            done = []
            for j in range(8):
                value = rows[j]
                for i in range(j):
                    value = value - s[j][i] * done[i]
                done.append(value * r[j])
            return done

        vx = forward([spread(v[p][j : j + 1, :]) for j in range(8)])
        new = vx[0]
        for j in range(1, 8):
            new = jnp.where(row == j, vx[j], new)
        v[p] = new
        if p == n - 1:
            break
        dx = forward([spread(d[p][j : j + 1, :]) for j in range(8)])
        for k in range(p + 1, n):
            factors = forward([spread(d[k][:, 8 * p + j : 8 * p + j + 1]) for j in range(8)])
            for j in range(8):
                d[k] = d[k] - factors[j] * dx[j]
                v[k] = v[k] - factors[j] * vx[j]
    return jnp.concatenate(v, axis=0)


def exact(a, b, contract=(((1,), (0,)), ((), ()))):
    return lax.dot_general(a, b, contract, precision=lax.Precision.HIGHEST, preferred_element_type=F32)


def basis_kernel(scale, tiles, a_ref, b_ref, r_ref, x_hbm, out_hbm, g, v, x_vmem, out_vmem, in_sem, out_sem):
    load = pltpu.make_async_copy(x_hbm, x_vmem, in_sem)
    load.start()
    core = lax.axis_index("core")
    g[pl.ds(pl.multiple_of(core * 384, 8), 384), :] = a_ref[...]
    g[pl.ds(pl.multiple_of((1 - core) * 384, 8), 384), :] = b_ref[...]

    def block(i):
        return g[i * 128 : (i + 1) * 128, :]

    m0 = inverse_factor(block(0))
    row0 = exact(m0, jnp.concatenate([block(1), block(2)], axis=1))
    minus = exact(row0, row0, CONTRACT0)
    left = -exact(row0, m0, CONTRACT0)
    m1 = inverse_factor(block(3) - minus[:128, :128])
    row1 = exact(m1, block(4) - minus[:128, 128:])
    m2 = inverse_factor(block(5) - minus[128:, 128:] - exact(row1, row1, CONTRACT0))
    v[...] = jnp.zeros((384, 384), F32)
    v[0:128, 0:128] = m0
    v10 = exact(m1, left[:128])
    v[128:256, 0:128] = v10
    v[128:256, 128:256] = m1
    v[256:384, 0:128] = exact(m2, left[128:] - exact(row1, v10, CONTRACT0))
    v[256:384, 128:256] = exact(m2, -exact(row1, m1, CONTRACT0))
    v[256:384, 256:384] = m2

    r = r_ref[...]
    w = sum(
        lax.dot_general(r, p, (((1,), (1,)), ((), ())), preferred_element_type=F32)
        for p in split(v[...], 3)
    )
    high, low = split(w * scale, 2)
    load.wait()
    size = x_vmem.shape[0] // tiles
    stores = []
    for i in range(tiles):
        at = pl.ds(i * size, size)
        x = x_vmem[at, :]
        out_vmem[at, :] = jnp.dot(x, high, preferred_element_type=F32) + jnp.dot(
            x, low, preferred_element_type=F32
        )
        store = pltpu.make_async_copy(out_vmem.at[at, :], out_hbm.at[at, :], out_sem.at[i])
        store.start()
        stores.append(store)
    for store in stores:
        store.wait()


def basis_of(scale, a, b, r, x):
    tiles = 6
    return pl.pallas_call(
        lambda *refs: basis_kernel(scale, tiles, *refs),
        in_specs=[VMEM, VMEM, VMEM, ANY],
        out_specs=ANY,
        out_shape=jax.ShapeDtypeStruct((x.shape[0], 384), F32),
        scratch_shapes=[
            pltpu.VMEM((768, 128), F32),
            pltpu.VMEM((384, 384), F32),
            pltpu.VMEM(x.shape, BF16),
            pltpu.VMEM((x.shape[0], 384), F32),
            pltpu.SemaphoreType.DMA,
            pltpu.SemaphoreType.DMA((tiles,)),
        ],
        compiler_params=pltpu.CompilerParams(vmem_limit_bytes=48 << 20),
    )(a, b, r, x)


def per_device(snapshots, range_test, corange_test):
    total = snapshots.shape[0] * 256
    swap = [(0, 1), (1, 0)]
    mine, other = products(snapshots, corange_test, range_test)
    pair = mine + lax.ppermute(other, "core", swap)
    got = lax.all_to_all(pair, PLANE, 0, 0, tiled=True)
    got = lax.all_to_all(column_blocks(got), COLUMN, 0, 0, tiled=True)
    gram, cosketch = plane_blocks(got)
    half = lax.all_to_all(gram, PLANE, 0, 0, tiled=True).reshape(384, 128)
    basis = basis_of(float(total) ** 0.5, half, lax.ppermute(half, "core", swap), range_test, snapshots)
    return basis, cosketch


def solution(mesh):
    fine = Mesh(mesh.devices.reshape(4, 2, 2, 4, 4), ROWS)
    in_specs = (P(ROWS, None), P(), P(ROWS, None))
    out_specs = (P(ROWS, None), P(("y", "zl", "core"), ("zh", "x")))
    return jax.shard_map(
        per_device, mesh=fine, in_specs=in_specs, out_specs=out_specs, check_vma=False
    )
```

```python
import jax
import jax.numpy as jnp
from jax import lax
from jax.experimental import pallas as pl
from jax.experimental.pallas import tpu as pltpu
from jax.sharding import Mesh, PartitionSpec as P

F32 = jnp.float32
BF16 = jnp.bfloat16
ROWS = ("y", "zl", "core", "zh", "x")
PLANE = ("y", "x")
COLUMN = ("zl", "zh")
VMEM = pl.BlockSpec(memory_space=pltpu.VMEM)
ANY = pl.BlockSpec(memory_space=pl.ANY)
HBM = pl.BlockSpec(memory_space=pltpu.HBM)
PRODUCTS_VMEM = 50 << 20
SUMS_VMEM = 8 << 20
BASIS_VMEM = 32 << 20
CONTRACT0 = (((0,), (0,)), ((), ()))
BLOCKS = ((0, 0), (0, 1), (0, 2), (1, 1), (1, 2), (2, 2))


def split(value, parts):
    pieces = []
    for _ in range(parts):
        piece = value.astype(BF16)
        pieces.append(piece)
        value = value - piece.astype(F32)
    return pieces


def lanes(shape):
    return lax.broadcasted_iota(jnp.int32, shape, len(shape) - 1)


def products_kernel(x_hbm, c_hbm, r_hbm, mine_ref, other_ref, x_ref, c_ref, r_ref, g_acc, p_acc, sems):
    rows = x_ref.shape[0]
    cuts = ((0, rows // 3), (rows // 3, rows))
    loads = []
    for start, end in cuts:
        at = pl.ds(start, end - start)
        loads.append((x_hbm.at[at, :], x_ref.at[at, :]))
    loads.append((r_hbm, r_ref))
    for start, end in cuts:
        at = pl.ds(start, end - start)
        loads.append((c_hbm.at[at, :], c_ref.at[at, :]))
    loads = [pltpu.make_async_copy(src, dst, sems.at[i]) for i, (src, dst) in enumerate(loads)]
    for load in loads:
        load.start()

    s = None
    for load, (start, end) in zip(loads[:2], cuts):
        load.wait()
        x = x_ref[start:end, :]
        part = lax.dot_general(x, x, CONTRACT0, preferred_element_type=F32)
        s = part if s is None else s + part
    loads[2].wait()
    r = r_ref[...]
    t = sum(jnp.dot(p, r, preferred_element_type=F32) for p in split(s, 3))
    pieces = split(t, 3)
    at = 0
    for i in range(3):
        left = r[:, i * 128 : (i + 1) * 128]
        row = sum(
            lax.dot_general(left, p[:, i * 128 :], CONTRACT0, preferred_element_type=F32)
            for p in pieces
        )
        for j in range(3 - i):
            g_acc[at * 128 : (at + 1) * 128, :] = row[:, j * 128 : (j + 1) * 128]
            at += 1
    k = None
    for load, (start, end) in zip(loads[3:], cuts):
        load.wait()
        part = lax.dot_general(
            c_ref[start:end, :], x_ref[start:end, :], CONTRACT0, preferred_element_type=F32
        )
        k = part if k is None else k + part
    quarter = lanes((768, 128)) // 32
    turned = [k[:, :128]]
    for zh in range(1, 4):
        turned.append(pltpu.roll(k[:, zh * 128 : (zh + 1) * 128], zh * 32, 1))
    for n in range(4):
        out = turned[0]
        for zh in range(1, 4):
            out = jnp.where(quarter == (n + zh) % 4, turned[zh], out)
        p_acc[n] = out
    core = lax.axis_index("core")
    for side, ref in ((1 - core, other_ref), (core, mine_ref)):
        for y in range(4):
            for n in range(4):
                peer = y * 4 + n
                ref[peer, 0:24, :] = g_acc[pl.ds(pl.multiple_of(side * 384 + peer * 24, 8), 24), :]
                for zl in range(2):
                    start = pl.multiple_of((y * 4 + zl * 2 + side) * 48, 8)
                    ref[peer, 24 + zl * 48 : 72 + zl * 48, :] = p_acc[n, pl.ds(start, 48), :]


def products(x, c, r):
    half = jax.ShapeDtypeStruct((16, 120, 128), F32)
    return pl.pallas_call(
        products_kernel,
        in_specs=[HBM, HBM, HBM],
        out_specs=(VMEM, VMEM),
        out_shape=(half, half),
        scratch_shapes=[
            pltpu.VMEM(x.shape, BF16),
            pltpu.VMEM(c.shape, BF16),
            pltpu.VMEM(r.shape, BF16),
            pltpu.VMEM((768, 128), F32),
            pltpu.VMEM((4, 768, 128), F32),
            pltpu.SemaphoreType.DMA((5,)),
        ],
        compiler_params=pltpu.CompilerParams(vmem_limit_bytes=PRODUCTS_VMEM),
    )(x, c, r)


def column_kernel(got_ref, out_ref):
    total = got_ref[0]
    for i in range(1, 16):
        total = total + got_ref[i]
    gram = total[0:24]
    shares = pltpu.roll(total[24:120], (4 - lax.axis_index("x")) % 4 * 32, 1)
    lane = lanes((16, 128)) // 32
    for zl in range(2):
        for zh in range(4):
            peer = zl * 4 + zh
            out_ref[peer, 0:24, :] = gram
            out = jnp.zeros((16, 128), F32)
            for q in range(3):
                start = zl * 48 + q * 16
                piece = shares[start : start + 16]
                shift = ((q - zh) * 32) % 128
                if shift:
                    piece = pltpu.roll(piece, shift, 1)
                out = jnp.where(lane == q, piece, out)
            out_ref[peer, 24:40, :] = out


def column_blocks(got):
    return pl.pallas_call(
        column_kernel,
        in_specs=[VMEM],
        out_specs=VMEM,
        out_shape=jax.ShapeDtypeStruct((8, 40, 128), F32),
        compiler_params=pltpu.CompilerParams(vmem_limit_bytes=SUMS_VMEM),
    )(got)


def plane_kernel(got_ref, gram_ref, cosketch_ref):
    total = got_ref[0]
    for i in range(1, 8):
        total = total + got_ref[i]
    for i in range(16):
        gram_ref[i] = total[0:24]
    share = total[24:40]
    rows = [share, pltpu.roll(share, 96, 1), pltpu.roll(share, 64, 1)]
    cosketch_ref[...] = jnp.concatenate(rows, axis=0).T[0:32, :]


def plane_blocks(got):
    return pl.pallas_call(
        plane_kernel,
        in_specs=[VMEM],
        out_specs=(VMEM, VMEM),
        out_shape=(
            jax.ShapeDtypeStruct((16, 24, 128), F32),
            jax.ShapeDtypeStruct((32, 48), F32),
        ),
        compiler_params=pltpu.CompilerParams(vmem_limit_bytes=SUMS_VMEM),
    )(got)


def spread(value):
    return jnp.broadcast_to(value, (8, 128))


def inverse_factor(block, same, beside=None):
    n, half = 16, 8
    d = [block[8 * i : 8 * i + 8, :] for i in range(n)]
    row = lax.broadcasted_iota(jnp.int32, (8, 128), 0)
    lane = lanes((8, 128))
    v = [jnp.where(lane == row + 8 * i, 1.0, 0.0).astype(F32) for i in range(n)]

    def stacked(rows):
        out = rows[0]
        for j in range(1, 8):
            out = jnp.where(row == j, rows[j], out)
        return out

    def columns_of(k, p):
        return [spread(d[k][:, 8 * p + j : 8 * p + j + 1]) for j in range(8)]

    def reader(values, at):
        for j, value in enumerate(values):
            same[at + 8 * j : at + 8 * j + 8, :] = value
        return lambda j, k: same[pl.ds(at + 8 * j + k, 8, stride=0), :]

    def rows_of(value, at):
        read = reader([value], at)
        return [read(0, j) for j in range(8)]

    own, u = columns_of(0, 0), []
    for p in range(n):
        base = (p % 2) * 160
        read = reader(own, base)
        s = [[read(j, k) if k >= j else None for j in range(8)] for k in range(8)]
        last = p == n - 1
        ahead = not last and p != half - 1
        if ahead:
            below, own = columns_of(p + 1, p), columns_of(p + 1, p + 1)
        r = []
        for j in range(8):
            r.append(lax.rsqrt(s[j][j]))
            for k in range(j + 1, 8):
                s[k][j] = s[k][j] * r[j]
            for m in range(j + 1, 8):
                for k in range(m, 8):
                    s[k][m] = s[k][m] - s[k][j] * s[m][j]

        def forward(rows):
            done = []
            for j in range(8):
                value = rows[j]
                for i in range(j):
                    value = value - s[j][i] * done[i]
                done.append(value * r[j])
            return done

        if ahead:
            below = forward(below)
            read = reader(below, base + 64)
            for m in range(8):
                for j in range(8):
                    own[m] = own[m] - below[j] * read(j, m)
        vx = forward(rows_of(v[p], base + 128))
        v[p] = stacked(vx)
        if not last:
            dx = forward(rows_of(d[p], base + 136))
            u.append(stacked(dx))
        if beside is not None:
            beside(p)
        for k in range(p + 1, half if p < half else n):
            factors = below if k == p + 1 else forward(columns_of(k, p))
            for j in range(8):
                d[k] = d[k] - factors[j] * dx[j]
                v[k] = v[k] - factors[j] * vx[j]
        if p == half - 1:
            top = jnp.concatenate(u, axis=0)
            both = jnp.where(lanes((64, 128)) < 64, jnp.concatenate(v[:half], axis=0), top)
            minus = exact(top, both, CONTRACT0)
            for k in range(half, n):
                part = minus[8 * k : 8 * k + 8]
                d[k] = d[k] - part
                v[k] = jnp.where(lane < 64, -part, v[k])
            own = columns_of(half, half)
    return jnp.concatenate(v, axis=0)


def exact(a, b, contract=(((1,), (0,)), ((), ()))):
    return lax.dot_general(a, b, contract, precision=lax.Precision.HIGHEST, preferred_element_type=F32)


def basis_kernel(scale, a_ref, b_ref, r_ref, x_hbm, out_hbm, g, x_vmem, out_vmem, same, in_sem, out_sem):
    load = pltpu.make_async_copy(x_hbm, x_vmem, in_sem)
    load.start()
    core = lax.axis_index("core")
    g[pl.ds(pl.multiple_of(core * 384, 8), 384), :] = a_ref[...]
    g[pl.ds(pl.multiple_of((1 - core) * 384, 8), 384), :] = b_ref[...]
    rows = x_vmem.shape[0]
    stores = []

    def block(i):
        return g[i * 128 : (i + 1) * 128, :]

    def columns(i, inverse, pieces, copies):
        left = r_ref[:, : inverse.shape[1]]
        weight = sum(
            lax.dot_general(left, p, (((1,), (1,)), ((), ())), preferred_element_type=F32)
            for p in split(inverse, 3)
        )
        weight = jnp.concatenate(split(weight * scale, 2), axis=1)
        size, every = rows // pieces, pieces // copies

        def piece(p):
            at = pl.ds(p * size, size)
            both = jnp.dot(x_vmem[at, :], weight, preferred_element_type=F32)
            out_vmem[i, at, :] = both[:, :128] + both[:, 128:]
            if p % every == every - 1:
                at = pl.ds((p + 1 - every) * size, every * size)
                store = pltpu.make_async_copy(
                    out_vmem.at[i, at, :],
                    out_hbm.at[at, pl.ds(i * 128, 128)],
                    out_sem.at[len(stores)],
                )
                store.start()
                stores.append(store)

        return piece

    m0 = inverse_factor(block(0), same)
    row0 = exact(m0, jnp.concatenate([block(1), block(2)], axis=1))
    minus = exact(row0, row0, CONTRACT0)
    left = -exact(row0, m0, CONTRACT0)
    load.wait()
    m1 = inverse_factor(block(3) - minus[:128, :128], same, columns(0, m0, 16, 2))
    row1 = exact(m1, block(4) - minus[:128, 128:])
    last = block(5) - minus[128:, 128:] - exact(row1, row1, CONTRACT0)
    v1 = jnp.concatenate([exact(m1, left[:128]), m1], axis=1)
    below = jnp.concatenate([left[128:], jnp.zeros((128, 128), F32)], axis=1) - exact(row1, v1, CONTRACT0)
    m2 = inverse_factor(last, same, columns(1, v1, 16, 2))
    piece = columns(2, jnp.concatenate([exact(m2, below), m2], axis=1), 4, 4)
    for p in range(4):
        piece(p)
    for store in stores:
        store.wait()


def basis_of(scale, a, b, r, x):
    return pl.pallas_call(
        lambda *refs: basis_kernel(scale, *refs),
        in_specs=[VMEM, VMEM, VMEM, ANY],
        out_specs=ANY,
        out_shape=jax.ShapeDtypeStruct((x.shape[0], 384), F32),
        scratch_shapes=[
            pltpu.VMEM((768, 128), F32),
            pltpu.VMEM(x.shape, BF16),
            pltpu.VMEM((3, x.shape[0], 128), F32),
            pltpu.VMEM((320, 128), F32),
            pltpu.SemaphoreType.DMA,
            pltpu.SemaphoreType.DMA((8,)),
        ],
        compiler_params=pltpu.CompilerParams(vmem_limit_bytes=BASIS_VMEM),
    )(a, b, r, x)


def per_device(snapshots, range_test, corange_test):
    total = snapshots.shape[0] * 256
    swap = [(0, 1), (1, 0)]
    mine, other = products(snapshots, corange_test, range_test)
    pair = mine + lax.ppermute(other, "core", swap)
    got = lax.all_to_all(pair, PLANE, 0, 0, tiled=True)
    got = lax.all_to_all(column_blocks(got), COLUMN, 0, 0, tiled=True)
    gram, cosketch = plane_blocks(got)
    half = lax.all_to_all(gram, PLANE, 0, 0, tiled=True).reshape(384, 128)
    basis = basis_of(float(total) ** 0.5, half, lax.ppermute(half, "core", swap), range_test, snapshots)
    return basis, cosketch.T


def solution(mesh):
    fine = Mesh(mesh.devices.reshape(4, 2, 2, 4, 4), ROWS)
    in_specs = (P(ROWS, None), P(), P(ROWS, None))
    out_specs = (P(ROWS, None), P(("y", "zl", "core"), ("zh", "x")))
    return jax.shard_map(
        per_device, mesh=fine, in_specs=in_specs, out_specs=out_specs, check_vma=False
    )
```

```python
import jax
import jax.numpy as jnp
from jax import lax
from jax.experimental import pallas as pl
from jax.experimental.pallas import tpu as pltpu
from jax.sharding import Mesh, PartitionSpec as P

F32 = jnp.float32
BF16 = jnp.bfloat16
ROWS = ("y", "zl", "core", "zh", "x")
PLANE = ("y", "x")
COLUMN = ("zl", "zh")
VMEM = pl.BlockSpec(memory_space=pltpu.VMEM)
ANY = pl.BlockSpec(memory_space=pl.ANY)
CORANGE_VMEM = 48 << 20
CORANGE_PARTS = 6
GRAM_VMEM = 32 << 20
SUMS_VMEM = 8 << 20
BASIS_VMEM = 32 << 20
CONTRACT0 = (((0,), (0,)), ((), ()))
BLOCKS = ((0, 0), (0, 1), (0, 2), (1, 1), (1, 2), (2, 2))


def split(value, parts):
    pieces = []
    for _ in range(parts):
        piece = value.astype(BF16)
        pieces.append(piece)
        value = value - piece.astype(F32)
    return pieces


def lanes(shape):
    return lax.broadcasted_iota(jnp.int32, shape, len(shape) - 1)


def loads_of(pairs, sems):
    loads = [pltpu.make_async_copy(src, dst, sems.at[i]) for i, (src, dst) in enumerate(pairs)]
    for load in loads:
        load.start()
    return loads


def cuts_of(rows, parts):
    return [pl.ds(i * rows // parts, rows // parts) for i in range(parts)]


def corange_kernel(x_hbm, c_hbm, mine_ref, other_ref, x_ref, c_ref, p_acc, sems):
    cuts = cuts_of(x_ref.shape[0], CORANGE_PARTS)
    pairs = []
    for at in cuts:
        pairs += [(x_hbm.at[at, :], x_ref.at[at, :]), (c_hbm.at[at, :], c_ref.at[at, :])]
    loads = loads_of(pairs, sems)
    k = None
    for i, at in enumerate(cuts):
        loads[2 * i].wait()
        loads[2 * i + 1].wait()
        part = lax.dot_general(c_ref[at, :], x_ref[at, :], CONTRACT0, preferred_element_type=F32)
        k = part if k is None else k + part
    quarter = lanes((768, 128)) // 32
    turned = [k[:, :128]]
    for zh in range(1, 4):
        turned.append(pltpu.roll(k[:, zh * 128 : (zh + 1) * 128], zh * 32, 1))
    for n in range(4):
        out = turned[0]
        for zh in range(1, 4):
            out = jnp.where(quarter == (n + zh) % 4, turned[zh], out)
        p_acc[n] = out
    core = lax.axis_index("core")
    for side, ref in ((1 - core, other_ref), (core, mine_ref)):
        for y in range(4):
            for n in range(4):
                for zl in range(2):
                    start = pl.multiple_of((y * 4 + zl * 2 + side) * 48, 8)
                    ref[y * 4 + n, zl * 48 : 48 + zl * 48, :] = p_acc[n, pl.ds(start, 48), :]


def corange_of(x, c):
    half = jax.ShapeDtypeStruct((16, 96, 128), F32)
    return pl.pallas_call(
        corange_kernel,
        in_specs=[ANY, ANY],
        out_specs=(VMEM, VMEM, VMEM),
        out_shape=(half, half, jax.ShapeDtypeStruct(x.shape, BF16)),
        scratch_shapes=[
            pltpu.VMEM(c.shape, BF16),
            pltpu.VMEM((4, 768, 128), F32),
            pltpu.SemaphoreType.DMA((2 * CORANGE_PARTS,)),
        ],
        compiler_params=pltpu.CompilerParams(vmem_limit_bytes=CORANGE_VMEM),
    )(x, c)


def gram_kernel(x_ref, r_ref, mine_ref, other_ref, g_acc):
    x = x_ref[...]
    s = lax.dot_general(x, x, CONTRACT0, preferred_element_type=F32)
    r = r_ref[...]
    t = sum(jnp.dot(p, r, preferred_element_type=F32) for p in split(s, 3))
    pieces = split(t, 3)
    at = 0
    for i in range(3):
        left = r[:, i * 128 : (i + 1) * 128]
        row = sum(
            lax.dot_general(left, p[:, i * 128 :], CONTRACT0, preferred_element_type=F32)
            for p in pieces
        )
        for j in range(3 - i):
            g_acc[at * 128 : (at + 1) * 128, :] = row[:, j * 128 : (j + 1) * 128]
            at += 1
    core = lax.axis_index("core")
    mine_ref[...] = g_acc[pl.ds(pl.multiple_of(core * 384, 8), 384), :]
    other_ref[...] = g_acc[pl.ds(pl.multiple_of((1 - core) * 384, 8), 384), :]


def gram_of(x, r):
    half = jax.ShapeDtypeStruct((384, 128), F32)
    return pl.pallas_call(
        gram_kernel,
        in_specs=[VMEM, VMEM],
        out_specs=(VMEM, VMEM),
        out_shape=(half, half),
        scratch_shapes=[pltpu.VMEM((768, 128), F32)],
        compiler_params=pltpu.CompilerParams(vmem_limit_bytes=GRAM_VMEM),
    )(x, r)


def pair_kernel(gram_ref, gram_got, share_ref, share_got, out_ref):
    for peer in range(16):
        at = pl.ds(peer * 24, 24)
        out_ref[peer, 0:24, :] = gram_ref[at, :] + gram_got[at, :]
        out_ref[peer, 24:120, :] = share_ref[peer] + share_got[peer]


def pair_blocks(*args):
    return pl.pallas_call(
        pair_kernel,
        in_specs=[VMEM] * 4,
        out_specs=VMEM,
        out_shape=jax.ShapeDtypeStruct((16, 120, 128), F32),
        compiler_params=pltpu.CompilerParams(vmem_limit_bytes=SUMS_VMEM),
    )(*args)


def column_kernel(got_ref, out_ref):
    total = got_ref[0]
    for i in range(1, 16):
        total = total + got_ref[i]
    gram = total[0:24]
    shares = pltpu.roll(total[24:120], (4 - lax.axis_index("x")) % 4 * 32, 1)
    lane = lanes((16, 128)) // 32
    for zl in range(2):
        for zh in range(4):
            peer = zl * 4 + zh
            out_ref[peer, 0:24, :] = gram
            out = jnp.zeros((16, 128), F32)
            for q in range(3):
                start = zl * 48 + q * 16
                piece = shares[start : start + 16]
                shift = ((q - zh) * 32) % 128
                if shift:
                    piece = pltpu.roll(piece, shift, 1)
                out = jnp.where(lane == q, piece, out)
            out_ref[peer, 24:40, :] = out


def column_blocks(got):
    return pl.pallas_call(
        column_kernel,
        in_specs=[VMEM],
        out_specs=VMEM,
        out_shape=jax.ShapeDtypeStruct((8, 40, 128), F32),
        compiler_params=pltpu.CompilerParams(vmem_limit_bytes=SUMS_VMEM),
    )(got)


def plane_kernel(got_ref, gram_ref, share_ref):
    total = got_ref[0]
    for i in range(1, 8):
        total = total + got_ref[i]
    for i in range(16):
        gram_ref[i] = total[0:24]
    share_ref[...] = total[24:40]


def plane_blocks(got):
    return pl.pallas_call(
        plane_kernel,
        in_specs=[VMEM],
        out_specs=(VMEM, VMEM),
        out_shape=(
            jax.ShapeDtypeStruct((16, 24, 128), F32),
            jax.ShapeDtypeStruct((16, 128), F32),
        ),
        compiler_params=pltpu.CompilerParams(vmem_limit_bytes=SUMS_VMEM),
    )(got)


def spread(value):
    return jnp.broadcast_to(value, (8, 128))


def inverse_factor(block, same, beside=None):
    n, half = 16, 8
    d = [block[8 * i : 8 * i + 8, :] for i in range(n)]
    row = lax.broadcasted_iota(jnp.int32, (8, 128), 0)
    lane = lanes((8, 128))
    v = [jnp.where(lane == row + 8 * i, 1.0, 0.0).astype(F32) for i in range(n)]

    def stacked(rows):
        out = rows[0]
        for j in range(1, 8):
            out = jnp.where(row == j, rows[j], out)
        return out

    def columns_of(k, p):
        return [spread(d[k][:, 8 * p + j : 8 * p + j + 1]) for j in range(8)]

    def reader(values, at):
        for j, value in enumerate(values):
            same[at + 8 * j : at + 8 * j + 8, :] = value
        return lambda j, k: same[pl.ds(at + 8 * j + k, 8, stride=0), :]

    def rows_of(value, at):
        read = reader([value], at)
        return [read(0, j) for j in range(8)]

    own, u = columns_of(0, 0), []
    for p in range(n):
        base = (p % 2) * 160
        read = reader(own, base)
        s = [[read(j, k) if k >= j else None for j in range(8)] for k in range(8)]
        last = p == n - 1
        ahead = not last and p != half - 1
        if ahead:
            below, own = columns_of(p + 1, p), columns_of(p + 1, p + 1)
        r = []
        for j in range(8):
            r.append(lax.rsqrt(s[j][j]))
            for k in range(j + 1, 8):
                s[k][j] = s[k][j] * r[j]
            for m in range(j + 1, 8):
                for k in range(m, 8):
                    s[k][m] = s[k][m] - s[k][j] * s[m][j]

        def forward(rows):
            done = []
            for j in range(8):
                value = rows[j]
                for i in range(j):
                    value = value - s[j][i] * done[i]
                done.append(value * r[j])
            return done

        if ahead:
            below = forward(below)
            read = reader(below, base + 64)
            for m in range(8):
                for j in range(8):
                    own[m] = own[m] - below[j] * read(j, m)
        vx = forward(rows_of(v[p], base + 128))
        v[p] = stacked(vx)
        if not last:
            dx = forward(rows_of(d[p], base + 136))
            u.append(stacked(dx))
        if beside is not None:
            beside(p)
        for k in range(p + 1, half if p < half else n):
            factors = below if k == p + 1 else forward(columns_of(k, p))
            for j in range(8):
                d[k] = d[k] - factors[j] * dx[j]
                v[k] = v[k] - factors[j] * vx[j]
        if p == half - 1:
            top = jnp.concatenate(u, axis=0)
            both = jnp.where(lanes((64, 128)) < 64, jnp.concatenate(v[:half], axis=0), top)
            minus = exact(top, both, CONTRACT0)
            for k in range(half, n):
                part = minus[8 * k : 8 * k + 8]
                d[k] = d[k] - part
                v[k] = jnp.where(lane < 64, -part, v[k])
            own = columns_of(half, half)
    return jnp.concatenate(v, axis=0)


def exact(a, b, contract=(((1,), (0,)), ((), ()))):
    return lax.dot_general(a, b, contract, precision=lax.Precision.HIGHEST, preferred_element_type=F32)


def basis_kernel(scale, a_ref, b_ref, share_ref, r_ref, x_ref, out_hbm, cosketch_ref, g, out_vmem, y_ref, same, out_sem):
    core = lax.axis_index("core")
    g[pl.ds(pl.multiple_of(core * 384, 8), 384), :] = a_ref[...]
    g[pl.ds(pl.multiple_of((1 - core) * 384, 8), 384), :] = b_ref[...]
    rows = x_ref.shape[0]
    stores = []

    def block(i):
        return g[i * 128 : (i + 1) * 128, :]

    def weight_of(inverse):
        left = r_ref[:, : inverse.shape[1]]
        weight = sum(
            lax.dot_general(left, p, (((1,), (1,)), ((), ())), preferred_element_type=F32)
            for p in split(inverse, 3)
        )
        return jnp.concatenate(split(weight, 2), axis=1)

    def times(left, weight):
        both = jnp.dot(left, weight, preferred_element_type=F32)
        return both[:, :128] + both[:, 128:]

    def columns(i, inverse, pieces, copies):
        weight = weight_of(inverse * scale)
        size, every = rows // pieces, pieces // copies

        def piece(p):
            at = pl.ds(p * size, size)
            out_vmem[i, at, :] = times(x_ref[at, :], weight)
            if p % every == every - 1:
                store(i, (p + 1 - every) * size, every * size)

        return piece

    def store(i, start, size):
        at = pl.ds(start, size)
        stores.append(
            pltpu.make_async_copy(
                out_vmem.at[i, at, :], out_hbm.at[at, pl.ds(i * 128, 128)], out_sem.at[len(stores)]
            )
        )
        stores[-1].start()

    share = share_ref[...]
    turned = [share, pltpu.roll(share, 96, 1), pltpu.roll(share, 64, 1)]
    cosketch_ref[...] = jnp.concatenate(turned, axis=0).T[0:32, :]
    m0 = inverse_factor(block(0), same)
    row0 = exact(m0, jnp.concatenate([block(1), block(2)], axis=1))
    minus = exact(row0, row0, CONTRACT0)
    left = -exact(row0, m0, CONTRACT0)
    m1 = inverse_factor(block(3) - minus[:128, :128], same, columns(0, m0, 16, 2))
    row1 = exact(m1, block(4) - minus[:128, 128:])
    last = block(5) - minus[128:, 128:] - exact(row1, row1, CONTRACT0)
    v1 = jnp.concatenate([exact(m1, left[:128]), m1], axis=1)
    below = jnp.concatenate([left[128:], jnp.zeros((128, 128), F32)], axis=1) - exact(row1, v1, CONTRACT0)
    one = jnp.where(lanes((128, 128)) == lax.broadcasted_iota(jnp.int32, (128, 128), 0), 1.0, 0.0)
    first = columns(1, v1, 16, 2)
    weight = weight_of(jnp.concatenate([below[:, :256], one.astype(F32)], axis=1))
    size = rows // 16

    def beside(p):
        first(p)
        at = pl.ds(p * size, size)
        y_ref[at, :] = jnp.concatenate(split(times(x_ref[at, :], weight), 2), axis=1)

    m2 = inverse_factor(last, same, beside)
    high, low = split(m2.T * scale, 2)
    weight = jnp.concatenate(
        [jnp.concatenate([high, low], axis=1), jnp.concatenate([high, jnp.zeros_like(low)], axis=1)], axis=0
    )
    size = rows // 4
    for p in range(4):
        at = pl.ds(p * size, size)
        out_vmem[2, at, :] = times(y_ref[at, :], weight)
        store(2, p * size, size)
    for copy in stores:
        copy.wait()


def basis_of(scale, a, b, share, r, x):
    return pl.pallas_call(
        lambda *refs: basis_kernel(scale, *refs),
        in_specs=[VMEM] * 5,
        out_specs=(ANY, VMEM),
        out_shape=(
            jax.ShapeDtypeStruct((x.shape[0], 384), F32),
            jax.ShapeDtypeStruct((32, 48), F32),
        ),
        scratch_shapes=[
            pltpu.VMEM((768, 128), F32),
            pltpu.VMEM((3, x.shape[0], 128), F32),
            pltpu.VMEM((x.shape[0], 256), BF16),
            pltpu.VMEM((320, 128), F32),
            pltpu.SemaphoreType.DMA((8,)),
        ],
        compiler_params=pltpu.CompilerParams(vmem_limit_bytes=BASIS_VMEM),
    )(a, b, share, r, x)


def per_device(snapshots, range_test, corange_test):
    total = snapshots.shape[0] * 256
    swap = [(0, 1), (1, 0)]
    share, share_out, held = corange_of(snapshots, corange_test)
    share_got = lax.ppermute(share_out, "core", swap)
    gram, gram_out = gram_of(held, range_test)
    gram_got = lax.ppermute(gram_out, "core", swap)
    pair = pair_blocks(gram, gram_got, share, share_got)
    got = lax.all_to_all(pair, PLANE, 0, 0, tiled=True)
    got = lax.all_to_all(column_blocks(got), COLUMN, 0, 0, tiled=True)
    gram, share = plane_blocks(got)
    half = lax.all_to_all(gram, PLANE, 0, 0, tiled=True).reshape(384, 128)
    other = lax.ppermute(half, "core", swap)
    basis, cosketch = basis_of(float(total) ** 0.5, half, other, share, range_test, held)
    return basis, cosketch.T


def solution(mesh):
    fine = Mesh(mesh.devices.reshape(4, 2, 2, 4, 4), ROWS)
    in_specs = (P(ROWS, None), P(), P(ROWS, None))
    out_specs = (P(ROWS, None), P(("y", "zl", "core"), ("zh", "x")))
    return jax.shard_map(
        per_device, mesh=fine, in_specs=in_specs, out_specs=out_specs, check_vma=False
    )
```

```python
import jax
import jax.numpy as jnp
from jax import lax
from jax.experimental import pallas as pl
from jax.experimental.pallas import tpu as pltpu
from jax.sharding import Mesh, PartitionSpec as P

F32 = jnp.float32
BF16 = jnp.bfloat16
ROWS = ("y", "zl", "core", "zh", "x")
PLANE = ("y", "x")
COLUMN = ("zl", "zh")
VMEM = pl.BlockSpec(memory_space=pltpu.VMEM)
ANY = pl.BlockSpec(memory_space=pl.ANY)
CORANGE_VMEM = 48 << 20
CORANGE_PARTS = 6
GRAM_VMEM = 32 << 20
SUMS_VMEM = 8 << 20
BASIS_VMEM = 32 << 20
CONTRACT0 = (((0,), (0,)), ((), ()))
BLOCKS = ((0, 0), (0, 1), (0, 2), (1, 1), (1, 2), (2, 2))


def split(value, parts):
    pieces = []
    for _ in range(parts):
        piece = value.astype(BF16)
        pieces.append(piece)
        value = value - piece.astype(F32)
    return pieces


def lanes(shape):
    return lax.broadcasted_iota(jnp.int32, shape, len(shape) - 1)


def loads_of(pairs, sems):
    loads = [pltpu.make_async_copy(src, dst, sems.at[i]) for i, (src, dst) in enumerate(pairs)]
    for load in loads:
        load.start()
    return loads


def cuts_of(rows, parts):
    return [pl.ds(i * rows // parts, rows // parts) for i in range(parts)]


def corange_kernel(x_hbm, c_hbm, mine_ref, other_ref, x_ref, c_ref, p_acc, sems):
    cuts = cuts_of(x_ref.shape[0], CORANGE_PARTS)
    pairs = []
    for at in cuts:
        pairs += [(x_hbm.at[at, :], x_ref.at[at, :]), (c_hbm.at[at, :], c_ref.at[at, :])]
    loads = loads_of(pairs, sems)
    k = None
    for i, at in enumerate(cuts):
        loads[2 * i].wait()
        loads[2 * i + 1].wait()
        part = lax.dot_general(c_ref[at, :], x_ref[at, :], CONTRACT0, preferred_element_type=F32)
        k = part if k is None else k + part
    quarter = lanes((768, 128)) // 32
    turned = [k[:, :128]]
    for zh in range(1, 4):
        turned.append(pltpu.roll(k[:, zh * 128 : (zh + 1) * 128], zh * 32, 1))
    for n in range(4):
        out = turned[0]
        for zh in range(1, 4):
            out = jnp.where(quarter == (n + zh) % 4, turned[zh], out)
        p_acc[n] = out
    core = lax.axis_index("core")
    for side, ref in ((1 - core, other_ref), (core, mine_ref)):
        for y in range(4):
            for n in range(4):
                for zl in range(2):
                    target = lax.rem(lax.axis_index("y") + y, 4)
                    start = pl.multiple_of((target * 4 + zl * 2 + side) * 48, 8)
                    at = (n * 2 + zl) * 48
                    ref[y, at : at + 48, :] = p_acc[n, pl.ds(start, 48), :]


def corange_of(x, c):
    half = jax.ShapeDtypeStruct((4, 384, 128), F32)
    return pl.pallas_call(
        corange_kernel,
        in_specs=[ANY, ANY],
        out_specs=(VMEM, VMEM, VMEM),
        out_shape=(half, half, jax.ShapeDtypeStruct(x.shape, BF16)),
        scratch_shapes=[
            pltpu.VMEM(c.shape, BF16),
            pltpu.VMEM((4, 768, 128), F32),
            pltpu.SemaphoreType.DMA((2 * CORANGE_PARTS,)),
        ],
        compiler_params=pltpu.CompilerParams(vmem_limit_bytes=CORANGE_VMEM),
    )(x, c)


def gram_kernel(x_ref, r_ref, mine_ref, other_ref, g_acc):
    x = x_ref[...]
    s = lax.dot_general(x, x, CONTRACT0, preferred_element_type=F32)
    r = r_ref[...]
    t = sum(jnp.dot(p, r, preferred_element_type=F32) for p in split(s, 3))
    pieces = split(t, 3)
    at = 0
    for i in range(3):
        left = r[:, i * 128 : (i + 1) * 128]
        row = sum(
            lax.dot_general(left, p[:, i * 128 :], CONTRACT0, preferred_element_type=F32)
            for p in pieces
        )
        for j in range(3 - i):
            g_acc[at * 128 : (at + 1) * 128, :] = row[:, j * 128 : (j + 1) * 128]
            at += 1
    core = lax.axis_index("core")
    mine_ref[...] = g_acc[pl.ds(pl.multiple_of(core * 384, 8), 384), :]
    other_ref[...] = g_acc[pl.ds(pl.multiple_of((1 - core) * 384, 8), 384), :]


def gram_of(x, r):
    half = jax.ShapeDtypeStruct((384, 128), F32)
    return pl.pallas_call(
        gram_kernel,
        in_specs=[VMEM, VMEM],
        out_specs=(VMEM, VMEM),
        out_shape=(half, half),
        scratch_shapes=[pltpu.VMEM((768, 128), F32)],
        compiler_params=pltpu.CompilerParams(vmem_limit_bytes=GRAM_VMEM),
    )(x, r)


def pair_kernel(share_ref, share_got, *shares):
    for y, ref in enumerate(shares):
        ref[...] = share_ref[y] + share_got[y]


def pair_shares(*args):
    share = jax.ShapeDtypeStruct((384, 128), F32)
    return pl.pallas_call(
        pair_kernel,
        in_specs=[VMEM] * 2,
        out_specs=(VMEM,) * 4,
        out_shape=(share,) * 4,
        compiler_params=pltpu.CompilerParams(vmem_limit_bytes=SUMS_VMEM),
    )(*args)


def column_kernel(got_ref, *refs):
    total = got_ref[0]
    for i in range(1, 16):
        total = total + got_ref[i]
    share = refs[0][...]
    for ref in refs[1:4]:
        share = share + ref[...]
    out_ref = refs[4]
    quarter = lanes((48, 128)) // 32
    for zl in range(2):
        for zh in range(4):
            peer = zl * 4 + zh
            out_ref[peer, 0:24, :] = total
            out = share[zl * 48 : zl * 48 + 48]
            for n in range(1, 4):
                at = (n * 2 + zl) * 48
                out = jnp.where(quarter == (n + zh) % 4, share[at : at + 48], out)
            out_ref[peer, 24:72, :] = out


def column_blocks(*args):
    return pl.pallas_call(
        column_kernel,
        in_specs=[VMEM] * 5,
        out_specs=VMEM,
        out_shape=jax.ShapeDtypeStruct((8, 72, 128), F32),
        compiler_params=pltpu.CompilerParams(vmem_limit_bytes=SUMS_VMEM),
    )(*args)


def plane_kernel(got_ref, out_ref):
    total = got_ref[0]
    for i in range(1, 8):
        total = total + got_ref[i]
    shares = pltpu.roll(total[24:72], (4 - lax.axis_index("zh")) % 4 * 32, 1)
    group = lanes((16, 128)) // 32
    for n in range(4):
        out = jnp.zeros((16, 128), F32)
        for q in range(3):
            piece = shares[q * 16 : q * 16 + 16]
            if q != n:
                piece = pltpu.roll(piece, (q - n) % 4 * 32, 1)
            out = jnp.where(group == q, piece, out)
        for y in range(4):
            out_ref[y * 4 + n, 0:24, :] = total[0:24]
            out_ref[y * 4 + n, 24:40, :] = out


def plane_blocks(got):
    return pl.pallas_call(
        plane_kernel,
        in_specs=[VMEM],
        out_specs=VMEM,
        out_shape=jax.ShapeDtypeStruct((16, 40, 128), F32),
        compiler_params=pltpu.CompilerParams(vmem_limit_bytes=SUMS_VMEM),
    )(got)


def spread(value):
    return jnp.broadcast_to(value, (8, 128))


def inverse_factor(block, same, beside=None):
    n, half = 16, 8
    e = [block[8 * i : 8 * i + 8, :] for i in range(n)]
    row = lax.broadcasted_iota(jnp.int32, (8, 128), 0)
    lane = lanes((8, 128))

    def stacked(rows):
        out = rows[0]
        for j in range(1, 8):
            out = jnp.where(row == j, rows[j], out)
        return out

    def columns_of(k, p):
        return [spread(e[k][:, 8 * p + j : 8 * p + j + 1]) for j in range(8)]

    def reader(values, at):
        for j, value in enumerate(values):
            same[at + 8 * j : at + 8 * j + 8, :] = value
        return lambda j, k: same[pl.ds(at + 8 * j + k, 8, stride=0), :]

    own = columns_of(0, 0)
    for p in range(n):
        base = (p % 2) * 160
        read = reader(own, base)
        s = [[read(j, k) if k >= j else None for j in range(8)] for k in range(8)]
        here = (lane >= 8 * p) & (lane < 8 * p + 8)
        ahead = p != n - 1 and p != half - 1
        if ahead:
            below, own = columns_of(p + 1, p), columns_of(p + 1, p + 1)
        r = []
        for j in range(8):
            r.append(lax.rsqrt(s[j][j]))
            for k in range(j + 1, 8):
                s[k][j] = s[k][j] * r[j]
            for m in range(j + 1, 8):
                for k in range(m, 8):
                    s[k][m] = s[k][m] - s[k][j] * s[m][j]

        def forward(rows):
            done = []
            for j in range(8):
                value = rows[j]
                for i in range(j):
                    value = value - s[j][i] * done[i]
                done.append(value * r[j])
            return done

        if ahead:
            below = forward(below)
            read = reader(below, base + 64)
            for m in range(8):
                for j in range(8):
                    own[m] = own[m] - below[j] * read(j, m)
        read = reader([jnp.where(here, jnp.where(lane == row + 8 * p, 1.0, 0.0), e[p])], base + 128)
        ex = forward([read(0, j) for j in range(8)])
        e[p] = stacked(ex)
        if beside is not None:
            beside(p)
        for k in range(p + 1, half if p < half else n):
            factors = below if k == p + 1 else forward(columns_of(k, p))
            e[k] = jnp.where(here, 0.0, e[k])
            for j in range(8):
                e[k] = e[k] - factors[j] * ex[j]
        if p == half - 1:
            top = jnp.concatenate(
                [jnp.where((lane > 8 * i + 7) & (lane < 64), 0.0, e[i]) for i in range(half)], axis=0
            )
            minus = exact(top, top, CONTRACT0)
            for k in range(half, n):
                e[k] = jnp.where(lane < 64, 0.0, e[k]) - minus[8 * k : 8 * k + 8]
            own = columns_of(half, half)
    return jnp.concatenate([jnp.where(lane > 8 * i + 7, 0.0, e[i]) for i in range(n)], axis=0)


def exact(a, b, contract=(((1,), (0,)), ((), ()))):
    return lax.dot_general(a, b, contract, precision=lax.Precision.HIGHEST, preferred_element_type=F32)


def basis_kernel(scale, a_ref, b_ref, got_ref, r_ref, x_ref, out_hbm, cosketch_hbm, g, out_vmem, y_ref, same, cosketch, cosketch_sem, out_sem):
    core = lax.axis_index("core")
    g[pl.ds(pl.multiple_of(core * 384, 8), 384), :] = a_ref[...]
    g[pl.ds(pl.multiple_of((1 - core) * 384, 8), 384), :] = b_ref[...]
    rows = x_ref.shape[0]
    y = lax.axis_index("y")
    share = got_ref[y * 4, 24:40, :]
    for n in range(1, 4):
        share = share + got_ref[y * 4 + n, 24:40, :]
    turned = [share, pltpu.roll(share, 96, 1), pltpu.roll(share, 64, 1)]
    cosketch[...] = jnp.concatenate(turned, axis=0).T[0:32, :]
    stores = [pltpu.make_async_copy(cosketch, cosketch_hbm, cosketch_sem)]
    stores[0].start()

    def block(i):
        return g[i * 128 : (i + 1) * 128, :]

    def weight_of(inverse):
        left = r_ref[:, : inverse.shape[1]]
        weight = sum(
            lax.dot_general(left, p, (((1,), (1,)), ((), ())), preferred_element_type=F32)
            for p in split(inverse, 3)
        )
        return jnp.concatenate(split(weight, 2), axis=1)

    def times(left, weight):
        both = jnp.dot(left, weight, preferred_element_type=F32)
        return both[:, :128] + both[:, 128:]

    def columns(i, inverse, pieces, copies):
        weight = weight_of(inverse * scale)
        size, every = rows // pieces, pieces // copies

        def piece(p):
            at = pl.ds(p * size, size)
            out_vmem[i, at, :] = times(x_ref[at, :], weight)
            if p % every == every - 1:
                store(i, (p + 1 - every) * size, every * size)

        return piece

    def store(i, start, size):
        at = pl.ds(start, size)
        stores.append(
            pltpu.make_async_copy(
                out_vmem.at[i, at, :], out_hbm.at[at, pl.ds(i * 128, 128)], out_sem.at[len(stores) - 1]
            )
        )
        stores[-1].start()

    m0 = inverse_factor(block(0), same)
    row0 = exact(m0, jnp.concatenate([block(1), block(2)], axis=1))
    minus = exact(row0, row0, CONTRACT0)
    left = -exact(row0, m0, CONTRACT0)
    m1 = inverse_factor(block(3) - minus[:128, :128], same, columns(0, m0, 16, 2))
    row1 = exact(m1, block(4) - minus[:128, 128:])
    last = block(5) - minus[128:, 128:] - exact(row1, row1, CONTRACT0)
    v1 = jnp.concatenate([exact(m1, left[:128]), m1], axis=1)
    below = jnp.concatenate([left[128:], jnp.zeros((128, 128), F32)], axis=1) - exact(row1, v1, CONTRACT0)
    one = jnp.where(lanes((128, 128)) == lax.broadcasted_iota(jnp.int32, (128, 128), 0), 1.0, 0.0)
    first = columns(1, v1, 16, 2)
    weight = weight_of(jnp.concatenate([below[:, :256], one.astype(F32)], axis=1))
    size = rows // 16

    def beside(p):
        first(p)
        at = pl.ds(p * size, size)
        y_ref[at, :] = jnp.concatenate(split(times(x_ref[at, :], weight), 2), axis=1)

    m2 = inverse_factor(last, same, beside)
    high, low = split(m2.T * scale, 2)
    weight = jnp.concatenate(
        [jnp.concatenate([high, low], axis=1), jnp.concatenate([high, jnp.zeros_like(low)], axis=1)], axis=0
    )
    size = rows // 4
    for p in range(4):
        at = pl.ds(p * size, size)
        out_vmem[2, at, :] = times(y_ref[at, :], weight)
        store(2, p * size, size)
    for copy in stores:
        copy.wait()


def basis_of(scale, a, b, got, r, x):
    return pl.pallas_call(
        lambda *refs: basis_kernel(scale, *refs),
        in_specs=[VMEM] * 5,
        out_specs=(ANY, ANY),
        out_shape=(
            jax.ShapeDtypeStruct((x.shape[0], 384), F32),
            jax.ShapeDtypeStruct((32, 48), F32),
        ),
        scratch_shapes=[
            pltpu.VMEM((768, 128), F32),
            pltpu.VMEM((3, x.shape[0], 128), F32),
            pltpu.VMEM((x.shape[0], 256), BF16),
            pltpu.VMEM((320, 128), F32),
            pltpu.VMEM((32, 48), F32),
            pltpu.SemaphoreType.DMA,
            pltpu.SemaphoreType.DMA((8,)),
        ],
        compiler_params=pltpu.CompilerParams(vmem_limit_bytes=BASIS_VMEM),
    )(a, b, got, r, x)


def per_device(snapshots, range_test, corange_test):
    total = snapshots.shape[0] * 256
    swap = [(0, 1), (1, 0)]
    share, share_out, held = corange_of(snapshots, corange_test)
    share_got = lax.ppermute(share_out, "core", swap)
    gram, gram_out = gram_of(held, range_test)
    gram_got = lax.ppermute(gram_out, "core", swap)
    shares = list(pair_shares(share, share_got))
    for shift in range(1, 4):
        shares[shift] = lax.ppermute(shares[shift], "y", [(y, (y + shift) % 4) for y in range(4)])
    pair = (gram + gram_got).reshape(16, 24, 128)
    got = lax.all_to_all(pair, PLANE, 0, 0, tiled=True)
    got = lax.all_to_all(column_blocks(got, *shares), COLUMN, 0, 0, tiled=True)
    got = lax.all_to_all(plane_blocks(got), PLANE, 0, 0, tiled=True)
    half = got[:, :24].reshape(384, 128)
    other = lax.ppermute(half, "core", swap)
    basis, cosketch = basis_of(float(total) ** 0.5, half, other, got, range_test, held)
    return basis, cosketch.T


def solution(mesh):
    fine = Mesh(mesh.devices.reshape(4, 2, 2, 4, 4), ROWS)
    in_specs = (P(ROWS, None), P(), P(ROWS, None))
    out_specs = (P(ROWS, None), P(("y", "zl", "core"), ("zh", "x")))
    return jax.shard_map(
        per_device, mesh=fine, in_specs=in_specs, out_specs=out_specs, check_vma=False
    )
```

```python
import jax
import jax.numpy as jnp
from jax import lax
from jax.experimental import pallas as pl
from jax.experimental.pallas import tpu as pltpu
from jax.sharding import Mesh, PartitionSpec as P

F32 = jnp.float32
BF16 = jnp.bfloat16
ROWS = ("y", "zl", "core", "zh", "x")
PLANE = ("y", "x")
COLUMN = ("zl", "zh")
VMEM = pl.BlockSpec(memory_space=pltpu.VMEM)
ANY = pl.BlockSpec(memory_space=pl.ANY)
CORANGE_VMEM = 48 << 20
CORANGE_PARTS = 6
GRAM_VMEM = 32 << 20
SUMS_VMEM = 8 << 20
BASIS_VMEM = 32 << 20
CONTRACT0 = (((0,), (0,)), ((), ()))
BLOCKS = ((0, 0), (0, 1), (0, 2), (1, 1), (1, 2), (2, 2))


def split(value, parts):
    pieces = []
    for _ in range(parts):
        piece = value.astype(BF16)
        pieces.append(piece)
        value = value - piece.astype(F32)
    return pieces


def lanes(shape):
    return lax.broadcasted_iota(jnp.int32, shape, len(shape) - 1)


def loads_of(pairs, sems):
    loads = [pltpu.make_async_copy(src, dst, sems.at[i]) for i, (src, dst) in enumerate(pairs)]
    for load in loads:
        load.start()
    return loads


def cuts_of(rows, parts):
    return [pl.ds(i * rows // parts, rows // parts) for i in range(parts)]


def corange_kernel(x_hbm, c_hbm, mine_ref, other_ref, x_ref, c_ref, p_acc, sems):
    cuts = cuts_of(x_ref.shape[0], CORANGE_PARTS)
    pairs = []
    for at in cuts:
        pairs += [(x_hbm.at[at, :], x_ref.at[at, :]), (c_hbm.at[at, :], c_ref.at[at, :])]
    loads = loads_of(pairs, sems)
    k = None
    for i, at in enumerate(cuts):
        loads[2 * i].wait()
        loads[2 * i + 1].wait()
        part = lax.dot_general(c_ref[at, :], x_ref[at, :], CONTRACT0, preferred_element_type=F32)
        k = part if k is None else k + part
    quarter = lanes((768, 128)) // 32
    turned = [k[:, :128]]
    for zh in range(1, 4):
        turned.append(pltpu.roll(k[:, zh * 128 : (zh + 1) * 128], zh * 32, 1))
    for n in range(4):
        out = turned[0]
        for zh in range(1, 4):
            out = jnp.where(quarter == (n + zh) % 4, turned[zh], out)
        p_acc[n] = out
    core = lax.axis_index("core")
    for side, ref in ((1 - core, other_ref), (core, mine_ref)):
        for y in range(4):
            for n in range(4):
                for zl in range(2):
                    target = lax.rem(lax.axis_index("y") + y, 4)
                    start = pl.multiple_of((target * 4 + zl * 2 + side) * 48, 8)
                    at = (n * 2 + zl) * 48
                    ref[y, at : at + 48, :] = p_acc[n, pl.ds(start, 48), :]


def corange_of(x, c):
    half = jax.ShapeDtypeStruct((4, 384, 128), F32)
    return pl.pallas_call(
        corange_kernel,
        in_specs=[ANY, ANY],
        out_specs=(VMEM, VMEM, VMEM),
        out_shape=(half, half, jax.ShapeDtypeStruct(x.shape, BF16)),
        scratch_shapes=[
            pltpu.VMEM(c.shape, BF16),
            pltpu.VMEM((4, 768, 128), F32),
            pltpu.SemaphoreType.DMA((2 * CORANGE_PARTS,)),
        ],
        compiler_params=pltpu.CompilerParams(vmem_limit_bytes=CORANGE_VMEM),
    )(x, c)


def gram_kernel(x_ref, r_ref, mine_ref, other_ref, g_acc):
    x = x_ref[...]
    s = lax.dot_general(x, x, CONTRACT0, preferred_element_type=F32)
    r = r_ref[...]
    t = sum(jnp.dot(p, r, preferred_element_type=F32) for p in split(s, 3))
    pieces = split(t, 3)
    at = 0
    for i in range(3):
        left = r[:, i * 128 : (i + 1) * 128]
        row = sum(
            lax.dot_general(left, p[:, i * 128 :], CONTRACT0, preferred_element_type=F32)
            for p in pieces
        )
        for j in range(3 - i):
            g_acc[at * 128 : (at + 1) * 128, :] = row[:, j * 128 : (j + 1) * 128]
            at += 1
    core = lax.axis_index("core")
    mine_ref[...] = g_acc[pl.ds(pl.multiple_of(core * 384, 8), 384), :]
    other_ref[...] = g_acc[pl.ds(pl.multiple_of((1 - core) * 384, 8), 384), :]


def gram_of(x, r):
    half = jax.ShapeDtypeStruct((384, 128), F32)
    return pl.pallas_call(
        gram_kernel,
        in_specs=[VMEM, VMEM],
        out_specs=(VMEM, VMEM),
        out_shape=(half, half),
        scratch_shapes=[pltpu.VMEM((768, 128), F32)],
        compiler_params=pltpu.CompilerParams(vmem_limit_bytes=GRAM_VMEM),
    )(x, r)


def pair_kernel(share_ref, share_got, *shares):
    for y, ref in enumerate(shares):
        ref[...] = share_ref[y] + share_got[y]


def pair_shares(*args):
    share = jax.ShapeDtypeStruct((384, 128), F32)
    return pl.pallas_call(
        pair_kernel,
        in_specs=[VMEM] * 2,
        out_specs=(VMEM,) * 4,
        out_shape=(share,) * 4,
        compiler_params=pltpu.CompilerParams(vmem_limit_bytes=SUMS_VMEM),
    )(*args)


def column_kernel(got_ref, *refs):
    total = got_ref[0]
    for i in range(1, 16):
        total = total + got_ref[i]
    share = refs[0][...]
    for ref in refs[1:4]:
        share = share + ref[...]
    out_ref = refs[4]
    quarter = lanes((48, 128)) // 32
    for zl in range(2):
        for zh in range(4):
            peer = zl * 4 + zh
            out_ref[peer, 0:24, :] = total
            out = share[zl * 48 : zl * 48 + 48]
            for n in range(1, 4):
                at = (n * 2 + zl) * 48
                out = jnp.where(quarter == (n + zh) % 4, share[at : at + 48], out)
            out_ref[peer, 24:72, :] = out


def column_blocks(*args):
    return pl.pallas_call(
        column_kernel,
        in_specs=[VMEM] * 5,
        out_specs=VMEM,
        out_shape=jax.ShapeDtypeStruct((8, 72, 128), F32),
        compiler_params=pltpu.CompilerParams(vmem_limit_bytes=SUMS_VMEM),
    )(*args)


def plane_kernel(got_ref, out_ref):
    total = got_ref[0]
    for i in range(1, 8):
        total = total + got_ref[i]
    shares = pltpu.roll(total[24:72], (4 - lax.axis_index("zh")) % 4 * 32, 1)
    group = lanes((16, 128)) // 32
    for n in range(4):
        out = jnp.zeros((16, 128), F32)
        for q in range(3):
            piece = shares[q * 16 : q * 16 + 16]
            if q != n:
                piece = pltpu.roll(piece, (q - n) % 4 * 32, 1)
            out = jnp.where(group == q, piece, out)
        for y in range(4):
            out_ref[y * 4 + n, 0:24, :] = total[0:24]
            out_ref[y * 4 + n, 24:40, :] = out


def plane_blocks(got):
    return pl.pallas_call(
        plane_kernel,
        in_specs=[VMEM],
        out_specs=VMEM,
        out_shape=jax.ShapeDtypeStruct((16, 40, 128), F32),
        compiler_params=pltpu.CompilerParams(vmem_limit_bytes=SUMS_VMEM),
    )(got)


def spread(value):
    return jnp.broadcast_to(value, (8, 128))


def inverse_factor(block, same, beside=None):
    n, half = 16, 8
    e = [block[8 * i : 8 * i + 8, :] for i in range(n)]
    row = lax.broadcasted_iota(jnp.int32, (8, 128), 0)
    lane = lanes((8, 128))

    def stacked(rows):
        out = rows[0]
        for j in range(1, 8):
            out = jnp.where(row == j, rows[j], out)
        return out

    def columns_of(k, p):
        return [spread(e[k][:, 8 * p + j : 8 * p + j + 1]) for j in range(8)]

    def reader(values, at):
        for j, value in enumerate(values):
            same[at + 8 * j : at + 8 * j + 8, :] = value
        return lambda j, k: same[pl.ds(at + 8 * j + k, 8, stride=0), :]

    own = columns_of(0, 0)
    for p in range(n):
        base = (p % 2) * 160
        read = reader(own, base)
        s = [[read(j, k) if k >= j else None for j in range(8)] for k in range(8)]
        here = (lane >= 8 * p) & (lane < 8 * p + 8)
        ahead = p != n - 1 and p != half - 1
        if ahead:
            below, own = columns_of(p + 1, p), columns_of(p + 1, p + 1)
        r = []
        for j in range(8):
            r.append(lax.rsqrt(s[j][j]))
            for k in range(j + 1, 8):
                s[k][j] = s[k][j] * r[j]
            for m in range(j + 1, 8):
                for k in range(m, 8):
                    s[k][m] = s[k][m] - s[k][j] * s[m][j]

        def forward(rows):
            done = []
            for j in range(8):
                value = rows[j]
                for i in range(j):
                    value = value - s[j][i] * done[i]
                done.append(value * r[j])
            return done

        if ahead:
            below = forward(below)
            read = reader(below, base + 64)
            for m in range(8):
                for j in range(8):
                    own[m] = own[m] - below[j] * read(j, m)
        read = reader([jnp.where(here, jnp.where(lane == row + 8 * p, 1.0, 0.0), e[p])], base + 128)
        ex = forward([read(0, j) for j in range(8)])
        e[p] = stacked(ex)
        if beside is not None:
            beside(p)
        for k in range(p + 1, half if p < half else n):
            factors = below if k == p + 1 else forward(columns_of(k, p))
            e[k] = jnp.where(here, 0.0, e[k])
            for j in range(8):
                e[k] = e[k] - factors[j] * ex[j]
        if p == half - 1:
            top = jnp.concatenate(
                [jnp.where((lane > 8 * i + 7) & (lane < 64), 0.0, e[i]) for i in range(half)], axis=0
            )
            minus = exact(top, top, CONTRACT0)
            for k in range(half, n):
                e[k] = jnp.where(lane < 64, 0.0, e[k]) - minus[8 * k : 8 * k + 8]
            own = columns_of(half, half)
    return jnp.concatenate([jnp.where(lane > 8 * i + 7, 0.0, e[i]) for i in range(n)], axis=0)


def exact(a, b, contract=(((1,), (0,)), ((), ()))):
    return lax.dot_general(a, b, contract, precision=lax.Precision.HIGHEST, preferred_element_type=F32)


def basis_kernel(scale, a_ref, b_ref, got_ref, r_ref, x_ref, out_hbm, cosketch_hbm, g, out_vmem, y_ref, same, cosketch, cosketch_sem, out_sem):
    core = lax.axis_index("core")
    g[pl.ds(pl.multiple_of(core * 384, 8), 384), :] = a_ref[...]
    g[pl.ds(pl.multiple_of((1 - core) * 384, 8), 384), :] = b_ref[...]
    rows = x_ref.shape[0]
    y = lax.axis_index("y")
    share = got_ref[y * 4, 24:40, :]
    for n in range(1, 4):
        share = share + got_ref[y * 4 + n, 24:40, :]
    turned = [share, pltpu.roll(share, 96, 1), pltpu.roll(share, 64, 1)]
    cosketch[...] = jnp.concatenate(turned, axis=0).T[0:32, :]
    stores = [pltpu.make_async_copy(cosketch, cosketch_hbm, cosketch_sem)]
    stores[0].start()

    def block(i):
        return g[i * 128 : (i + 1) * 128, :]

    def weight_of(inverse):
        left = r_ref[:, : inverse.shape[1]]
        weight = sum(
            lax.dot_general(left, p, (((1,), (1,)), ((), ())), preferred_element_type=F32)
            for p in split(inverse, 3)
        )
        return jnp.concatenate(split(weight, 2), axis=1)

    def times(left, weight):
        both = jnp.dot(left, weight, preferred_element_type=F32)
        return both[:, :128] + both[:, 128:]

    def columns(i, inverse, pieces, copies):
        weight = weight_of(inverse * scale)
        size, every = rows // pieces, pieces // copies

        def piece(p):
            at = pl.ds(p * size, size)
            out_vmem[i, at, :] = times(x_ref[at, :], weight)
            if p % every == every - 1:
                store(i, (p + 1 - every) * size, every * size)

        return piece

    def store(i, start, size):
        at = pl.ds(start, size)
        stores.append(
            pltpu.make_async_copy(
                out_vmem.at[i, at, :], out_hbm.at[at, pl.ds(i * 128, 128)], out_sem.at[len(stores) - 1]
            )
        )
        stores[-1].start()

    m0 = inverse_factor(block(0), same)
    row0 = exact(m0, jnp.concatenate([block(1), block(2)], axis=1))
    minus = exact(row0, row0, CONTRACT0)
    left = -exact(row0, m0, CONTRACT0)
    m1 = inverse_factor(block(3) - minus[:128, :128], same, columns(0, m0, 16, 2))
    row1 = exact(m1, block(4) - minus[:128, 128:])
    last = block(5) - minus[128:, 128:] - exact(row1, row1, CONTRACT0)
    v1 = jnp.concatenate([exact(m1, left[:128]), m1], axis=1)
    below = jnp.concatenate([left[128:], jnp.zeros((128, 128), F32)], axis=1) - exact(row1, v1, CONTRACT0)
    one = jnp.where(lanes((128, 128)) == lax.broadcasted_iota(jnp.int32, (128, 128), 0), 1.0, 0.0)
    first = columns(1, v1, 16, 2)
    weight = weight_of(jnp.concatenate([below[:, :256], one.astype(F32)], axis=1))
    size = rows // 16

    def beside(p):
        first(p)
        at = pl.ds(p * size, size)
        y_ref[at, :] = jnp.concatenate(split(times(x_ref[at, :], weight), 2), axis=1)

    m2 = inverse_factor(last, same, beside)
    high, low = split(m2.T * scale, 2)
    weight = jnp.concatenate(
        [jnp.concatenate([high, low], axis=1), jnp.concatenate([high, jnp.zeros_like(low)], axis=1)], axis=0
    )
    size = rows // 6
    for p in range(6):
        at = pl.ds(p * size, size)
        out_vmem[2, at, :] = times(y_ref[at, :], weight)
        store(2, p * size, size)
    for copy in stores:
        copy.wait()


def basis_of(scale, a, b, got, r, x):
    return pl.pallas_call(
        lambda *refs: basis_kernel(scale, *refs),
        in_specs=[VMEM] * 5,
        out_specs=(ANY, ANY),
        out_shape=(
            jax.ShapeDtypeStruct((x.shape[0], 384), F32),
            jax.ShapeDtypeStruct((32, 48), F32),
        ),
        scratch_shapes=[
            pltpu.VMEM((768, 128), F32),
            pltpu.VMEM((3, x.shape[0], 128), F32),
            pltpu.VMEM((x.shape[0], 256), BF16),
            pltpu.VMEM((320, 128), F32),
            pltpu.VMEM((32, 48), F32),
            pltpu.SemaphoreType.DMA,
            pltpu.SemaphoreType.DMA((10,)),
        ],
        compiler_params=pltpu.CompilerParams(vmem_limit_bytes=BASIS_VMEM),
    )(a, b, got, r, x)


def per_device(snapshots, range_test, corange_test):
    total = snapshots.shape[0] * 256
    swap = [(0, 1), (1, 0)]
    share, share_out, held = corange_of(snapshots, corange_test)
    share_got = lax.ppermute(share_out, "core", swap)
    gram, gram_out = gram_of(held, range_test)
    gram_got = lax.ppermute(gram_out, "core", swap)
    shares = list(pair_shares(share, share_got))
    for shift in range(1, 4):
        shares[shift] = lax.ppermute(shares[shift], "y", [(y, (y + shift) % 4) for y in range(4)])
    pair = (gram + gram_got).reshape(16, 24, 128)
    got = lax.all_to_all(pair, PLANE, 0, 0, tiled=True)
    got = lax.all_to_all(column_blocks(got, *shares), COLUMN, 0, 0, tiled=True)
    got = lax.all_to_all(plane_blocks(got), PLANE, 0, 0, tiled=True)
    half = got[:, :24].reshape(384, 128)
    other = lax.ppermute(half, "core", swap)
    basis, cosketch = basis_of(float(total) ** 0.5, half, other, got, range_test, held)
    return basis, cosketch.T


def solution(mesh):
    fine = Mesh(mesh.devices.reshape(4, 2, 2, 4, 4), ROWS)
    in_specs = (P(ROWS, None), P(), P(ROWS, None))
    out_specs = (P(ROWS, None), P(("y", "zl", "core"), ("zh", "x")))
    return jax.shard_map(
        per_device, mesh=fine, in_specs=in_specs, out_specs=out_specs, check_vma=False
    )
```
